32 devices in a mesh: row: 16 (over z, x, core), col: 2 (over y).
Axes of the slice: x: 2, y: 2, z: 4, core: 2. Of those that a mesh axis runs over, the one named last changes fastest.
Arguments:
- series: float32 [2, 262144], P(None, 'row'), may hold values from -6 to 6
- exclusion: int32 [1], replicated, may hold values from 8 to 48
- col_starts: int32 [2], P('col'), may hold values from 0 to 261632, as said below
Outputs:
- row_profile: float32 [262144], P('row')
- col_profile: float32 [1024], P('col')
The draws below stay inside these ranges and needn't reach their ends.
Inputs may be any that keep to these rules, and one draw needn't show every extreme that they name: `col_starts`: each a multiple of 512; one of them is 261632.
All inputs are finite; a program needn't handle non-finite values.
Results may differ from the reference program's by a relative error of at most 0.0014.
Values may be sent and summed in bfloat16 or wider, within the bound.
A program may use at most 64 MiB of HBM per device.

```python
import jax
import jax.numpy as jnp
from jax import lax

CHANNELS = 2
WINDOW = 64
TR = 16384
TC = 512
ROWS = 262144
BAND = 1024


def draw_col_starts(key, part):
    tile_count = BAND // TC
    starts = jax.random.randint(key, (tile_count,), 0, ROWS // TC, dtype=jnp.int32) * TC
    last_slot = jax.random.randint(jax.random.fold_in(key, 17), (), 0, tile_count, dtype=jnp.int32)
    return jnp.where(jnp.arange(tile_count, dtype=jnp.int32) == last_slot, jnp.int32(ROWS - TC), starts)


def levels(own_key, shape, cuts, smallest, top_value):
    gain = 1.0
    for position, parts in cuts:
        steps = jax.random.uniform(jax.random.fold_in(jax.random.fold_in(own_key, 6), position), (parts,), jnp.float32, smallest / len(cuts), top_value / len(cuts))
        gain = gain * jnp.repeat(jnp.exp(steps), shape[position] // parts).reshape((-1,) + (1,) * (len(shape) - 1 - position))
    return gain


def noise(key, shape, scale, reach, split=(), kind=jnp.bfloat16):
    values = jax.random.normal(key, shape, jnp.float32) * scale
    if len(split) > 0:
        values = levels(key, shape, split, -0.22, 0.18) * values
    return jnp.clip(values, min=-reach, max=reach).astype(kind)


def setup_inputs(seed: int = 0) -> dict:
    splits = jax.random.split(jax.random.key(seed), 4)
    return {
        "series": noise(splits[0], (CHANNELS, ROWS), 1.0, 6.0, ((1, 16),), jnp.float32),
        "exclusion": jax.random.randint(splits[1], (1,), 8, 49).astype(jnp.int32),
        "col_starts": draw_col_starts(jax.random.fold_in(splits[3], 71), 0),
    }


def normalised_windows(segment, win_count):
    channels = segment.shape[0]
    lags = segment.shape[1] - win_count + 1
    stacked = jnp.stack([segment[:, lag_index:lag_index + win_count] for lag_index in range(lags)], axis=-1)
    centred = stacked - lax.optimization_barrier(jnp.mean(stacked, axis=-1, keepdims=True))
    spread = lax.optimization_barrier(jnp.mean(centred * centred, axis=-1, keepdims=True))
    scaled = centred / jnp.sqrt(channels * lags * (spread + 1e-05))
    return jnp.transpose(scaled, (1, 0, 2)).reshape(win_count, channels * lags).astype(jnp.bfloat16)

def reference(series, exclusion, col_starts):
    channels = series.shape[0]
    total = series.shape[1]
    padded = jnp.concatenate([series, jnp.zeros((channels, WINDOW - 1), jnp.float32)], axis=1)
    all_windows = normalised_windows(padded, total)
    tile_count = BAND // TC
    col_windows = jnp.concatenate([lax.dynamic_slice_in_dim(all_windows, col_starts[tile_index].astype(jnp.int32), TC, 0) for tile_index in range(tile_count)], axis=0)
    col_ids = jnp.concatenate([col_starts[tile_index].astype(jnp.int32) + jnp.arange(TC, dtype=jnp.int32) for tile_index in range(tile_count)])
    valid_count = total - WINDOW + 1
    zone_width = exclusion[0].astype(jnp.int32)
    last_col = jnp.max(col_ids)
    block_count = total // TR
    blocks = all_windows.reshape(block_count, TR, all_windows.shape[1])
    firsts = jnp.arange(block_count, dtype=jnp.int32) * TR

    def row_block_step(best_cols, pair):
        block, first_row = pair

        def block_maxima(unused):
            scores = jnp.dot(block, col_windows.T, preferred_element_type=jnp.float32)
            row_ids = first_row + jnp.arange(TR, dtype=jnp.int32)
            kept_mask = (col_ids[None, :] - row_ids[:, None] >= zone_width) & (col_ids < valid_count)[None, :]
            masked = jnp.where(kept_mask, scores, jnp.float32(-1.0))
            return (lax.optimization_barrier(jnp.max(masked, axis=1)), lax.optimization_barrier(jnp.max(masked, axis=0)))

        def masked_block(unused):
            return (jnp.full((TR,), -1.0, jnp.float32), jnp.full((BAND,), -1.0, jnp.float32))
        row_part, col_part = lax.cond(last_col - first_row < zone_width, masked_block, block_maxima, 0)
        return (jnp.maximum(best_cols, col_part), row_part)
    start_best = jnp.full((BAND,), -1.0, jnp.float32)
    best_cols, row_parts = lax.scan(row_block_step, start_best, (blocks, firsts))
    return (row_parts.reshape(total), best_cols)
```

```python
import functools

import jax
import jax.numpy as jnp
from jax import lax
from jax.experimental import pallas as pl
from jax.experimental.pallas import tpu as pltpu
from jax.sharding import PartitionSpec as P

WINDOW = 64
TC = 512
LANES = 128
CHUNK = TC
EDGE = TC + LANES
SPAN = EDGE + LANES
MASKED = -4.0
MESH = pl.DeviceIdType.MESH


def normalised(x, count):
    channels, length = x.shape
    parts = []
    for channel in range(channels):
        line = jnp.broadcast_to(x[channel : channel + 1], (8, length))
        fan = pltpu.roll(line, length - 7, 1, stride=1, stride_axis=0)
        groups = [fan[:, 8 * g : 8 * g + count] for g in range(WINDOW // 8)]
        total = functools.reduce(jnp.add, groups)
        mean = jnp.sum(total, axis=0, keepdims=True) * (1.0 / WINDOW)
        groups = [g - mean for g in groups]
        square = functools.reduce(jnp.add, [g * g for g in groups])
        spread = jnp.sum(square, axis=0, keepdims=True) * (1.0 / WINDOW)
        scale = 1.0 / jnp.sqrt(channels * WINDOW * (spread + 1e-05))
        parts += [g * scale for g in groups]
    return jnp.concatenate(parts, axis=0)


def kernel(
    R, C, N, pieces,
    series, exclusion, col_starts,
    row_out, col_out,
    seg_all, row_all, col_all, rows, cols, edge, best,
    seg_send, seg_recv, col_send, col_recv, row_send, row_recv,
):
    r, c = lax.axis_index("row"), lax.axis_index("col")
    barrier = pltpu.get_barrier_semaphore()

    @pl.loop(1, R)
    def _(d):
        pl.semaphore_signal(
            barrier, inc=1, device_id=(lax.rem(r + d, R), c), device_id_type=MESH
        )

    @pl.loop(1, C)
    def _(d):
        pl.semaphore_signal(
            barrier, inc=1, device_id=(r, lax.rem(c + d, C)), device_id_type=MESH
        )

    col_first = col_starts[0]
    start = col_first - r * N

    before = jnp.zeros((2, LANES), jnp.float32)
    body = jnp.zeros((2, TC), jnp.float32)
    after = jnp.zeros((2, LANES), jnp.float32)
    for first in range(0, N, TC):
        part = series[:, first : first + TC]
        away = jnp.full((2, TC), start - first)
        body = jnp.where(away == 0, part, body)
        before = jnp.where(away[:, :LANES] == TC, part[:, TC - LANES :], before)
        after = jnp.where(away[:, :LANES] == -TC, part[:, :LANES], after)
    seg_all[r, :, 0:LANES] = before
    seg_all[r, :, LANES : LANES + TC] = body
    seg_all[r, :, LANES + TC : SPAN] = after
    seg_all[r, :, SPAN:] = series[:, 0:LANES]
    pl.semaphore_wait(barrier, R + C - 2)

    def seg_copy(d):
        return pltpu.make_async_remote_copy(
            src_ref=seg_all.at[r], dst_ref=seg_all.at[r],
            send_sem=seg_send.at[d], recv_sem=seg_recv.at[d],
            device_id=(lax.rem(r + d, R), c), device_id_type=MESH,
        )

    def col_copy(d):
        return pltpu.make_async_remote_copy(
            src_ref=col_all.at[r], dst_ref=col_all.at[r],
            send_sem=col_send.at[d], recv_sem=col_recv.at[d],
            device_id=(lax.rem(r + d, R), c), device_id_type=MESH,
        )

    span = N // pieces

    def row_copy(d, piece):
        part = row_all.at[c, :, pl.ds(piece * span, span)]
        return pltpu.make_async_remote_copy(
            src_ref=part, dst_ref=part,
            send_sem=row_send.at[d, piece], recv_sem=row_recv.at[d, piece],
            device_id=(r, lax.rem(c + d, C)), device_id_type=MESH,
        )

    @pl.loop(1, R)
    def _(d):
        seg_copy(d).start()

    @pl.loop(0, N // CHUNK - 1)
    def _(step):
        first = pl.multiple_of(step * CHUNK, CHUNK)
        block = normalised(series[:, pl.ds(first, CHUNK + LANES)], CHUNK)
        rows[:, pl.ds(first, CHUNK)] = block.astype(jnp.bfloat16)

    @pl.loop(1, R)
    def _(d):
        seg_copy(d).wait()

    rim = seg_all[lax.rem(r + 1, R), :, SPAN:]
    rim = jnp.where(r == R - 1, 0.0, rim)
    tail = jnp.concatenate([series[:, N - CHUNK :], rim], axis=1)
    rows[:, N - CHUNK :] = normalised(tail, CHUNK).astype(jnp.bfloat16)

    around = normalised(jnp.sum(seg_all[:, :, :SPAN], axis=0), EDGE)
    cols[:, :LANES] = around[:, LANES:].T.astype(jnp.bfloat16)
    around = around.astype(jnp.bfloat16)
    place = col_first + lax.broadcasted_iota(jnp.int32, (TC, LANES), 0)
    last = jnp.where(place <= R * N - WINDOW, place - exclusion[0], -1)
    lane = lax.broadcasted_iota(jnp.int32, (TC, LANES), 1)
    cut = jnp.where(lane * LANES + (r * N + LANES - 1) > last, MASKED, 0.0)
    cols[:, LANES:] = cut.astype(jnp.bfloat16)

    col_best = jnp.full((TC, LANES), -1.0, jnp.float32)
    edges = []
    for g in range(EDGE // LANES):
        block = around[:, g * LANES : (g + 1) * LANES]
        scores = jnp.dot(cols[:, :LANES], block, preferred_element_type=jnp.float32)
        row = col_first + ((g - 1) * LANES) + lane
        scores = jnp.where((row <= last) & (row >= 0), scores, -1.0)
        col_best = jnp.maximum(col_best, scores)
        edges.append(jnp.max(scores, axis=0, keepdims=True))
    best[...] = col_best
    low = jnp.full((1, CHUNK - LANES), -1.0, jnp.float32)
    edge[0] = jnp.concatenate(edges[1:], axis=1)
    edge[1] = jnp.concatenate([low, edges[0]], axis=1)

    group = lax.broadcasted_iota(jnp.int32, (LANES, CHUNK), 0)
    owned = lax.broadcasted_iota(jnp.int32, (LANES, CHUNK), 1) // LANES

    def step_rows(step):
        first = pl.multiple_of(step * CHUNK, CHUNK)
        mark = jnp.where(group - owned == step * (CHUNK // LANES), 1.0, 0.0)
        right = jnp.concatenate([rows[:, pl.ds(first, CHUNK)], mark.astype(jnp.bfloat16)], axis=0)
        scores = jnp.dot(cols[...], right, preferred_element_type=jnp.float32)
        part = scores[:, :LANES]
        for g in range(1, CHUNK // LANES):
            part = jnp.maximum(part, scores[:, g * LANES : (g + 1) * LANES])
        best[...] = jnp.maximum(best[...], part)
        row_best = jnp.max(scores, axis=0, keepdims=True)
        away = jnp.full((1, CHUNK), col_starts[0] - r * N - first)
        row_best = jnp.maximum(row_best, jnp.where(away == 0, edge[0], -1.0))
        row_best = jnp.maximum(row_best, jnp.where(away == CHUNK, edge[1], -1.0))
        row_all[c, :, pl.ds(first, CHUNK)] = row_best

    per_piece = N // CHUNK // pieces
    for piece in range(pieces):
        pl.loop(piece * per_piece, (piece + 1) * per_piece)(step_rows)

        @pl.loop(1, C)
        def _(d):
            row_copy(d, piece).start()

    col_all[r] = jnp.max(best[...].T, axis=0, keepdims=True)

    @pl.loop(1, R)
    def _(d):
        col_copy(d).start()

    @pl.loop(1, C)
    def _(d):
        for piece in range(pieces):
            row_copy(d, piece).wait()

    row_out[...] = functools.reduce(jnp.maximum, [row_all[k] for k in range(C)])

    @pl.loop(1, R)
    def _(d):
        col_copy(d).wait()

    col_out[...] = jnp.max(col_all[...], axis=0)


def local(R, C, series, exclusion, col_starts):
    channels, N = series.shape
    pieces = 4
    vmem, smem = pl.BlockSpec(memory_space=pltpu.VMEM), pl.BlockSpec(memory_space=pltpu.SMEM)
    dma = pltpu.SemaphoreType.DMA
    row_best, col_best = pl.pallas_call(
        functools.partial(kernel, R, C, N, pieces),
        out_shape=(
            jax.ShapeDtypeStruct((1, N), jnp.float32),
            jax.ShapeDtypeStruct((1, TC), jnp.float32),
        ),
        in_specs=[vmem, smem, smem],
        out_specs=(vmem, vmem),
        scratch_shapes=[
            pltpu.VMEM((R, channels, SPAN + LANES), jnp.float32),
            pltpu.VMEM((C, 1, N), jnp.float32),
            pltpu.VMEM((R, 1, TC), jnp.float32),
            pltpu.VMEM((channels * WINDOW, N), jnp.bfloat16),
            pltpu.VMEM((TC, 2 * LANES), jnp.bfloat16),
            pltpu.VMEM((2, 1, CHUNK), jnp.float32),
            pltpu.VMEM((TC, LANES), jnp.float32),
            dma((R,)), dma((R,)), dma((R,)), dma((R,)),
            dma((C, pieces)), dma((C, pieces)),
        ],
        compiler_params=pltpu.CompilerParams(
            collective_id=0, has_side_effects=True, vmem_limit_bytes=40 * 1024 * 1024
        ),
    )(series, exclusion, col_starts)
    return row_best.reshape(N), col_best.reshape(TC)


def solution(mesh):
    placed = (P(None, "row"), P(), P("col"))
    R, C = mesh.shape["row"], mesh.shape["col"]
    return jax.shard_map(
        functools.partial(local, R, C),
        mesh=mesh,
        in_specs=placed,
        out_specs=(P("row"), P("col")),
        check_vma=False,
    )
```

```python
import functools

import jax
import jax.numpy as jnp
from jax import lax
from jax.experimental import pallas as pl
from jax.experimental.pallas import tpu as pltpu
from jax.sharding import PartitionSpec as P

WINDOW = 64
TC = 512
LANES = 128
CHUNK = TC
EDGE = TC + LANES
SPAN = EDGE + LANES
MASKED = -4.0
MESH = pl.DeviceIdType.MESH


def normalised(x, count):
    channels, length = x.shape
    parts = []
    for channel in range(channels):
        line = jnp.broadcast_to(x[channel : channel + 1], (8, length))
        groups = [
            pltpu.roll(line, length - 7 - 8 * g, 1, stride=1, stride_axis=0)[:, :count]
            for g in range(WINDOW // 8)
        ]
        total = functools.reduce(jnp.add, groups)
        mean = jnp.sum(total, axis=0, keepdims=True) * (1.0 / WINDOW)
        groups = [g - mean for g in groups]
        square = functools.reduce(jnp.add, [g * g for g in groups])
        spread = jnp.sum(square, axis=0, keepdims=True) * (1.0 / WINDOW)
        scale = 1.0 / jnp.sqrt(channels * WINDOW * (spread + 1e-05))
        parts += [g * scale for g in groups]
    return jnp.concatenate(parts, axis=0)


def kernel(
    R, C, N, pieces,
    series, exclusion, col_starts,
    row_out, col_out,
    seg_all, row_all, col_all, rows, cols, edge, best,
    seg_send, seg_recv, col_send, col_recv, row_send, row_recv,
):
    r, c = lax.axis_index("row"), lax.axis_index("col")
    barrier = pltpu.get_barrier_semaphore()

    @pl.loop(1, R)
    def _(d):
        pl.semaphore_signal(
            barrier, inc=1, device_id=(lax.rem(r + d, R), c), device_id_type=MESH
        )

    @pl.loop(1, C)
    def _(d):
        pl.semaphore_signal(
            barrier, inc=1, device_id=(r, lax.rem(c + d, C)), device_id_type=MESH
        )

    col_first = col_starts[0]
    start = col_first - r * N

    before = jnp.zeros((2, LANES), jnp.float32)
    body = jnp.zeros((2, TC), jnp.float32)
    after = jnp.zeros((2, LANES), jnp.float32)
    for first in range(0, N, TC):
        part = series[:, first : first + TC]
        away = jnp.full((2, TC), start - first)
        body = jnp.where(away == 0, part, body)
        before = jnp.where(away[:, :LANES] == TC, part[:, TC - LANES :], before)
        after = jnp.where(away[:, :LANES] == -TC, part[:, :LANES], after)
    seg_all[r, :, 0:LANES] = before
    seg_all[r, :, LANES : LANES + TC] = body
    seg_all[r, :, LANES + TC : SPAN] = after
    seg_all[r, :, SPAN:] = series[:, 0:LANES]
    pl.semaphore_wait(barrier, R + C - 2)

    def seg_copy(d):
        return pltpu.make_async_remote_copy(
            src_ref=seg_all.at[r], dst_ref=seg_all.at[r],
            send_sem=seg_send.at[d], recv_sem=seg_recv.at[d],
            device_id=(lax.rem(r + d, R), c), device_id_type=MESH,
        )

    def col_copy(d):
        return pltpu.make_async_remote_copy(
            src_ref=col_all.at[r], dst_ref=col_all.at[r],
            send_sem=col_send.at[d], recv_sem=col_recv.at[d],
            device_id=(lax.rem(r + d, R), c), device_id_type=MESH,
        )

    span = N // pieces

    def row_copy(d, piece):
        part = row_all.at[c, :, pl.ds(piece * span, span)]
        return pltpu.make_async_remote_copy(
            src_ref=part, dst_ref=part,
            send_sem=row_send.at[d, piece], recv_sem=row_recv.at[d, piece],
            device_id=(r, lax.rem(c + d, C)), device_id_type=MESH,
        )

    @pl.loop(1, R)
    def _(d):
        seg_copy(d).start()

    def rows_of(step):
        first = step * CHUNK if isinstance(step, int) else pl.multiple_of(step * CHUNK, CHUNK)
        block = normalised(series[:, pl.ds(first, CHUNK + LANES)], CHUNK)
        rows[:, pl.ds(first, CHUNK)] = block.astype(jnp.bfloat16)

    whole = (N // CHUNK - 1) // 2

    @pl.loop(0, whole)
    def _(step):
        for k in range(2):
            rows_of(step * 2 + k)

    for k in range(whole * 2, N // CHUNK - 1):
        rows_of(k)

    @pl.loop(1, R)
    def _(d):
        seg_copy(d).wait()

    rim = seg_all[lax.rem(r + 1, R), :, SPAN:]
    rim = jnp.where(r == R - 1, 0.0, rim)
    tail = jnp.concatenate([series[:, N - CHUNK :], rim], axis=1)
    rows[:, N - CHUNK :] = normalised(tail, CHUNK).astype(jnp.bfloat16)

    around = normalised(jnp.sum(seg_all[:, :, :SPAN], axis=0), EDGE)
    cols[:, :LANES] = around[:, LANES:].T.astype(jnp.bfloat16)
    around = around.astype(jnp.bfloat16)
    place = col_first + lax.broadcasted_iota(jnp.int32, (TC, LANES), 0)
    last = jnp.where(place <= R * N - WINDOW, place - exclusion[0], -1)
    lane = lax.broadcasted_iota(jnp.int32, (TC, LANES), 1)
    cut = jnp.where(lane * LANES + (r * N + LANES - 1) > last, MASKED, 0.0)
    cols[:, LANES:] = cut.astype(jnp.bfloat16)

    col_best = jnp.full((TC, LANES), -1.0, jnp.float32)
    edges = []
    for g in range(EDGE // LANES):
        block = around[:, g * LANES : (g + 1) * LANES]
        scores = jnp.dot(cols[:, :LANES], block, preferred_element_type=jnp.float32)
        row = col_first + ((g - 1) * LANES) + lane
        scores = jnp.where((row <= last) & (row >= 0), scores, -1.0)
        col_best = jnp.maximum(col_best, scores)
        edges.append(jnp.max(scores, axis=0, keepdims=True))
    best[...] = col_best
    low = jnp.full((1, CHUNK - LANES), -1.0, jnp.float32)
    edge[0] = jnp.concatenate(edges[1:], axis=1)
    edge[1] = jnp.concatenate([low, edges[0]], axis=1)

    group = lax.broadcasted_iota(jnp.int32, (LANES, CHUNK), 0)
    owned = lax.broadcasted_iota(jnp.int32, (LANES, CHUNK), 1) // LANES

    def step_rows(step):
        first = pl.multiple_of(step * CHUNK, CHUNK)
        mark = jnp.where(group - owned == step * (CHUNK // LANES), 1.0, 0.0)
        right = jnp.concatenate([rows[:, pl.ds(first, CHUNK)], mark.astype(jnp.bfloat16)], axis=0)
        scores = jnp.dot(cols[...], right, preferred_element_type=jnp.float32)
        part = scores[:, :LANES]
        for g in range(1, CHUNK // LANES):
            part = jnp.maximum(part, scores[:, g * LANES : (g + 1) * LANES])
        best[...] = jnp.maximum(best[...], part)
        row_best = jnp.max(scores, axis=0, keepdims=True)
        away = jnp.full((1, CHUNK), col_starts[0] - r * N - first)
        row_best = jnp.maximum(row_best, jnp.where(away == 0, edge[0], -1.0))
        row_best = jnp.maximum(row_best, jnp.where(away == CHUNK, edge[1], -1.0))
        row_all[c, :, pl.ds(first, CHUNK)] = row_best

    per_piece = N // CHUNK // pieces
    for piece in range(pieces):
        @pl.loop(0, per_piece // 4)
        def _(step):
            for k in range(4):
                step_rows(piece * per_piece + step * 4 + k)


        @pl.loop(1, C)
        def _(d):
            row_copy(d, piece).start()

    col_all[r] = jnp.max(best[...].T, axis=0, keepdims=True)

    @pl.loop(1, R)
    def _(d):
        col_copy(d).start()

    @pl.loop(1, C)
    def _(d):
        for piece in range(pieces):
            row_copy(d, piece).wait()

    row_out[...] = functools.reduce(jnp.maximum, [row_all[k] for k in range(C)])

    @pl.loop(1, R)
    def _(d):
        col_copy(d).wait()

    col_out[...] = jnp.max(col_all[...], axis=0)


def local(R, C, series, exclusion, col_starts):
    channels, N = series.shape
    pieces = 4
    vmem, smem = pl.BlockSpec(memory_space=pltpu.VMEM), pl.BlockSpec(memory_space=pltpu.SMEM)
    dma = pltpu.SemaphoreType.DMA
    row_best, col_best = pl.pallas_call(
        functools.partial(kernel, R, C, N, pieces),
        out_shape=(
            jax.ShapeDtypeStruct((1, N), jnp.float32),
            jax.ShapeDtypeStruct((1, TC), jnp.float32),
        ),
        in_specs=[vmem, smem, smem],
        out_specs=(vmem, vmem),
        scratch_shapes=[
            pltpu.VMEM((R, channels, SPAN + LANES), jnp.float32),
            pltpu.VMEM((C, 1, N), jnp.float32),
            pltpu.VMEM((R, 1, TC), jnp.float32),
            pltpu.VMEM((channels * WINDOW, N), jnp.bfloat16),
            pltpu.VMEM((TC, 2 * LANES), jnp.bfloat16),
            pltpu.VMEM((2, 1, CHUNK), jnp.float32),
            pltpu.VMEM((TC, LANES), jnp.float32),
            dma((R,)), dma((R,)), dma((R,)), dma((R,)),
            dma((C, pieces)), dma((C, pieces)),
        ],
        compiler_params=pltpu.CompilerParams(
            collective_id=0, has_side_effects=True, vmem_limit_bytes=40 * 1024 * 1024
        ),
    )(series, exclusion, col_starts)
    return row_best.reshape(N), col_best.reshape(TC)


def solution(mesh):
    placed = (P(None, "row"), P(), P("col"))
    R, C = mesh.shape["row"], mesh.shape["col"]
    return jax.shard_map(
        functools.partial(local, R, C),
        mesh=mesh,
        in_specs=placed,
        out_specs=(P("row"), P("col")),
        check_vma=False,
    )
```

```python
import functools

import jax
import jax.numpy as jnp
from jax import lax
from jax.experimental import pallas as pl
from jax.experimental.pallas import tpu as pltpu
from jax.sharding import PartitionSpec as P

WINDOW = 64
TC = 512
LANES = 128
CHUNK = TC
EDGE = TC + LANES
SPAN = EDGE + LANES
MASKED = -4.0
MESH = pl.DeviceIdType.MESH


def normalised(x, count):
    channels, length = x.shape
    parts = []
    for channel in range(channels):
        line = jnp.broadcast_to(x[channel : channel + 1], (8, length))
        groups = [
            pltpu.roll(line, length - 7 - 8 * g, 1, stride=1, stride_axis=0)[:, :count]
            for g in range(WINDOW // 8)
        ]
        total = functools.reduce(jnp.add, groups)
        mean = jnp.sum(total, axis=0, keepdims=True) * (1.0 / WINDOW)
        groups = [g - mean for g in groups]
        square = functools.reduce(jnp.add, [g * g for g in groups])
        spread = jnp.sum(square, axis=0, keepdims=True) * (1.0 / WINDOW)
        scale = 1.0 / jnp.sqrt(channels * WINDOW * (spread + 1e-05))
        parts += [g * scale for g in groups]
    return jnp.concatenate(parts, axis=0)


def kernel(
    R, C, N, pieces,
    series, exclusion, col_starts,
    row_out, col_out,
    seg_all, row_all, col_all, rows, cols, edge, best,
    seg_send, seg_recv, col_send, col_recv, row_send, row_recv,
):
    r, c = lax.axis_index("row"), lax.axis_index("col")
    barrier = pltpu.get_barrier_semaphore()

    @pl.loop(1, R)
    def _(d):
        pl.semaphore_signal(
            barrier, inc=1, device_id=(lax.rem(r + d, R), c), device_id_type=MESH
        )

    @pl.loop(1, C)
    def _(d):
        pl.semaphore_signal(
            barrier, inc=1, device_id=(r, lax.rem(c + d, C)), device_id_type=MESH
        )

    col_first = col_starts[0]
    start = col_first - r * N

    before = jnp.zeros((2, LANES), jnp.float32)
    body = jnp.zeros((2, TC), jnp.float32)
    after = jnp.zeros((2, LANES), jnp.float32)
    for first in range(0, N, TC):
        part = series[:, first : first + TC]
        away = jnp.full((2, TC), start - first)
        body = jnp.where(away == 0, part, body)
        before = jnp.where(away[:, :LANES] == TC, part[:, TC - LANES :], before)
        after = jnp.where(away[:, :LANES] == -TC, part[:, :LANES], after)
    seg_all[r, :, 0:LANES] = before
    seg_all[r, :, LANES : LANES + TC] = body
    seg_all[r, :, LANES + TC : SPAN] = after
    seg_all[r, :, SPAN:] = series[:, 0:LANES]
    pl.semaphore_wait(barrier, R + C - 2)

    def seg_copy(d):
        return pltpu.make_async_remote_copy(
            src_ref=seg_all.at[r], dst_ref=seg_all.at[r],
            send_sem=seg_send.at[d], recv_sem=seg_recv.at[d],
            device_id=(lax.rem(r + d, R), c), device_id_type=MESH,
        )

    def col_copy(d):
        return pltpu.make_async_remote_copy(
            src_ref=col_all.at[r], dst_ref=col_all.at[r],
            send_sem=col_send.at[d], recv_sem=col_recv.at[d],
            device_id=(lax.rem(r + d, R), c), device_id_type=MESH,
        )

    span = N // pieces

    def row_copy(d, piece):
        part = row_all.at[c, :, pl.ds(piece * span, span)]
        return pltpu.make_async_remote_copy(
            src_ref=part, dst_ref=part,
            send_sem=row_send.at[d, piece], recv_sem=row_recv.at[d, piece],
            device_id=(r, lax.rem(c + d, C)), device_id_type=MESH,
        )

    @pl.loop(1, R)
    def _(d):
        seg_copy(d).start()

    def rows_of(step):
        first = step * CHUNK if isinstance(step, int) else pl.multiple_of(step * CHUNK, CHUNK)
        block = normalised(series[:, pl.ds(first, CHUNK + LANES)], CHUNK)
        rows[:, pl.ds(first, CHUNK)] = block.astype(jnp.bfloat16)

    whole = (N // CHUNK - 1) // 2

    @pl.loop(0, whole)
    def _(step):
        for k in range(2):
            rows_of(step * 2 + k)

    for k in range(whole * 2, N // CHUNK - 1):
        rows_of(k)

    @pl.loop(1, R)
    def _(d):
        seg_copy(d).wait()

    rim = seg_all[lax.rem(r + 1, R), :, SPAN:]
    rim = jnp.where(r == R - 1, 0.0, rim)
    tail = jnp.concatenate([series[:, N - CHUNK :], rim], axis=1)
    rows[:, N - CHUNK :] = normalised(tail, CHUNK).astype(jnp.bfloat16)

    around = normalised(jnp.sum(seg_all[:, :, :SPAN], axis=0), EDGE)
    cols[:, :LANES] = around[:, LANES:].T.astype(jnp.bfloat16)
    around = around.astype(jnp.bfloat16)
    place = col_first + lax.broadcasted_iota(jnp.int32, (TC, LANES), 0)
    last = jnp.where(place <= R * N - WINDOW, place - exclusion[0], -1)
    lane = lax.broadcasted_iota(jnp.int32, (TC, LANES), 1)
    cut = jnp.where(lane * LANES + (r * N + LANES - 1) > last, MASKED, 0.0)
    cols[:, LANES:] = cut.astype(jnp.bfloat16)

    col_best = jnp.full((TC, LANES), -1.0, jnp.float32)
    edges = []
    for g in range(EDGE // LANES):
        block = around[:, g * LANES : (g + 1) * LANES]
        scores = jnp.dot(cols[:, :LANES], block, preferred_element_type=jnp.float32)
        row = col_first + ((g - 1) * LANES) + lane
        scores = jnp.where((row <= last) & (row >= 0), scores, -1.0)
        col_best = jnp.maximum(col_best, scores)
        edges.append(jnp.max(scores, axis=0, keepdims=True))
    best[...] = col_best
    low = jnp.full((1, CHUNK - LANES), -1.0, jnp.float32)
    edge[0] = jnp.concatenate(edges[1:], axis=1)
    edge[1] = jnp.concatenate([low, edges[0]], axis=1)

    group = lax.broadcasted_iota(jnp.int32, (LANES, CHUNK), 0)
    owned = lax.broadcasted_iota(jnp.int32, (LANES, CHUNK), 1) // LANES

    def step_rows(step):
        first = pl.multiple_of(step * CHUNK, CHUNK)
        mark = jnp.where(group - owned == step * (CHUNK // LANES), 1.0, 0.0)
        right = jnp.concatenate([rows[:, pl.ds(first, CHUNK)], mark.astype(jnp.bfloat16)], axis=0)
        scores = jnp.dot(cols[...], right, preferred_element_type=jnp.float32)
        part = scores[:, :LANES]
        for g in range(1, CHUNK // LANES):
            part = jnp.maximum(part, scores[:, g * LANES : (g + 1) * LANES])
        best[...] = jnp.maximum(best[...], part)
        row_best = jnp.max(scores, axis=0, keepdims=True)
        away = jnp.full((1, CHUNK), col_starts[0] - r * N - first)
        row_best = jnp.maximum(row_best, jnp.where(away == 0, edge[0], -1.0))
        row_best = jnp.maximum(row_best, jnp.where(away == CHUNK, edge[1], -1.0))
        row_all[c, :, pl.ds(first, CHUNK)] = row_best

    per_piece = N // CHUNK // pieces
    unit = 8 if per_piece % 8 == 0 else 1
    for piece in range(pieces):
        @pl.loop(0, per_piece // unit)
        def _(step):
            for k in range(unit):
                step_rows(piece * per_piece + step * unit + k)


        @pl.loop(1, C)
        def _(d):
            row_copy(d, piece).start()

    col_all[r] = jnp.max(best[...].T, axis=0, keepdims=True)

    @pl.loop(1, R)
    def _(d):
        col_copy(d).start()

    @pl.loop(1, C)
    def _(d):
        for piece in range(pieces):
            row_copy(d, piece).wait()

    row_out[...] = functools.reduce(jnp.maximum, [row_all[k] for k in range(C)])

    @pl.loop(1, R)
    def _(d):
        col_copy(d).wait()

    col_out[...] = jnp.max(col_all[...], axis=0)


def local(R, C, series, exclusion, col_starts):
    channels, N = series.shape
    pieces = 4
    vmem, smem = pl.BlockSpec(memory_space=pltpu.VMEM), pl.BlockSpec(memory_space=pltpu.SMEM)
    dma = pltpu.SemaphoreType.DMA
    row_best, col_best = pl.pallas_call(
        functools.partial(kernel, R, C, N, pieces),
        out_shape=(
            jax.ShapeDtypeStruct((1, N), jnp.float32),
            jax.ShapeDtypeStruct((1, TC), jnp.float32),
        ),
        in_specs=[vmem, smem, smem],
        out_specs=(vmem, vmem),
        scratch_shapes=[
            pltpu.VMEM((R, channels, SPAN + LANES), jnp.float32),
            pltpu.VMEM((C, 1, N), jnp.float32),
            pltpu.VMEM((R, 1, TC), jnp.float32),
            pltpu.VMEM((channels * WINDOW, N), jnp.bfloat16),
            pltpu.VMEM((TC, 2 * LANES), jnp.bfloat16),
            pltpu.VMEM((2, 1, CHUNK), jnp.float32),
            pltpu.VMEM((TC, LANES), jnp.float32),
            dma((R,)), dma((R,)), dma((R,)), dma((R,)),
            dma((C, pieces)), dma((C, pieces)),
        ],
        compiler_params=pltpu.CompilerParams(
            collective_id=0, has_side_effects=True, vmem_limit_bytes=40 * 1024 * 1024
        ),
    )(series, exclusion, col_starts)
    return row_best.reshape(N), col_best.reshape(TC)


def solution(mesh):
    placed = (P(None, "row"), P(), P("col"))
    R, C = mesh.shape["row"], mesh.shape["col"]
    return jax.shard_map(
        functools.partial(local, R, C),
        mesh=mesh,
        in_specs=placed,
        out_specs=(P("row"), P("col")),
        check_vma=False,
    )
```
